32 devices in a mesh: section: 16 (over z, x, core), tensor: 2 (over y).
Axes of the slice: x: 2, y: 2, z: 4, core: 2. Of those that a mesh axis runs over, the one named last changes fastest.
Arguments:
- activations: bfloat16 [16, 256, 4096], P('section', 'tensor'), may hold values from -6 to 6
- upstream_grad: bfloat16 [16, 256, 4096], P('section', 'tensor'), may hold values from -6 to 6
- stash_blocks: bfloat16 [16, 256, 4096], P('section', 'tensor'), may hold values from -6 to 6
- guest_blocks: bfloat16 [16, 256, 4096], P('section', 'tensor'), may hold values from -6 to 6
- norm_gain: float32 [16, 4096], P('section'), may hold values from 0.1 to 1.9
- query_weight: bfloat16 [16, 4096, 4096], P('section', None, 'tensor'), may hold values from -2 to 2
- keyval_weight: bfloat16 [16, 4096, 2, 1024], P('section', None, None, 'tensor'), may hold values from -1 to 1
- output_weight: bfloat16 [16, 4096, 4096], P('section', 'tensor'), may hold values from -0.09375 to 0.09375
- evict_marks: int32 [16, 16], replicated, may hold values from 0 to 1, as said below
Outputs:
- next_input: bfloat16 [16, 256, 4096], P('section', 'tensor')
- prev_grad: bfloat16 [16, 256, 4096], P('section', 'tensor')
- kept_stash: bfloat16 [16, 256, 4096], P('section', 'tensor')
- held_blocks: bfloat16 [16, 256, 4096], P('section', 'tensor')
The draws below stay inside these ranges and needn't reach their ends.
Inputs may be any that keep to these rules, and one draw needn't show every extreme that they name: `evict_marks`: row s marks with 1 the blocks that section s evicts to section 15 - s; a row has at most 8 ones, row 0 exactly 8, rows of the first half of the sections at least 4.
All inputs are finite; a program needn't handle non-finite values.
Results may differ from the reference program's by a relative error of at most 0.012.
Values may be sent and summed in bfloat16 or wider, within the bound.
No kernel may reach another device: no remote copies, remote signals or barrier semaphores. Data moves between devices by JAX's collectives and lax.ppermute only.
A program may use at most 128 MiB of HBM per device.

```python
import math
import jax
import jax.numpy as jnp
from jax import lax

WIDTH = 4096
HEADS = 32
KV_HEADS = 8
HEAD_DIM = 128
TOK = 256
BLOCKS = 16
MOST_EVICT = 8
SECTIONS = 16
N_TENSOR = 2


def weight_pair(key):
    keyval_key = jax.random.fold_in(key, 11)
    query_key = jax.random.fold_in(key, 12)
    keyval = jax.random.normal(keyval_key, (SECTIONS, WIDTH, 2, KV_HEADS * HEAD_DIM), jnp.float32) / math.sqrt(WIDTH)
    noise_part = jax.random.normal(query_key, (SECTIONS, WIDTH, HEADS * HEAD_DIM), jnp.float32) / math.sqrt(WIDTH)
    return (keyval, noise_part)


def draw_keyval_weight(key, part):
    keyval, noise_part = weight_pair(key)
    return keyval.astype(jnp.bfloat16)


def draw_query_weight(key, part):
    keyval, noise_part = weight_pair(key)
    return noise_part.astype(jnp.bfloat16)


def draw_evict_marks(key, part):
    count_key = jax.random.fold_in(key, 21)
    order_key = jax.random.fold_in(key, 22)
    base_count = jax.random.randint(count_key, (SECTIONS,), 0, MOST_EVICT // 2 + 1)
    early_extra = jnp.where(jnp.arange(SECTIONS) < SECTIONS // 2, MOST_EVICT - MOST_EVICT // 2, 0)
    counts = jnp.minimum(base_count + early_extra, MOST_EVICT)
    counts = counts.at[0].set(MOST_EVICT)
    block_order = jax.vmap(lambda section_key: jax.random.permutation(section_key, BLOCKS))(jax.random.split(order_key, SECTIONS))
    return (block_order < counts[:, None]).astype(jnp.int32)


def steps_of(own_key, dims, cuts, least, top_value):
    loudness, own = 1.0, jax.random.fold_in(own_key, 6)
    for dim, shards_of in cuts:
        draws = jnp.exp(jax.random.uniform(jax.random.fold_in(own, dim), (shards_of,), jnp.float32, least / len(cuts), top_value / len(cuts)))
        loudness = loudness * jnp.repeat(draws, dims[dim] // shards_of).reshape([-1 if axis == dim else 1 for axis in range(len(dims))])
    return loudness


def gaussian(own_key, dims, scale, bound, pieces=(), held_as=jnp.bfloat16):
    level = steps_of(own_key, dims, pieces, -0.22, 0.18) if pieces else 1.0
    result = jax.random.normal(own_key, dims, jnp.float32) * scale * level
    return jnp.minimum(jnp.maximum(result, -bound), bound).astype(held_as)


def setup_inputs(seed: int = 0) -> dict:
    splits = jax.random.split(jax.random.key(seed), 10)
    return {
        "activations": gaussian(splits[0], (SECTIONS, TOK, WIDTH), 1.0, 6.0, ((0, 16), (1, 2))),
        "upstream_grad": gaussian(splits[1], (SECTIONS, TOK, WIDTH), 1.0, 6.0, ((0, 16), (1, 2))),
        "stash_blocks": gaussian(splits[2], (SECTIONS, TOK, WIDTH), 1.0, 6.0, ((0, 16), (1, 2))),
        "guest_blocks": gaussian(splits[3], (SECTIONS, TOK, WIDTH), 1.0, 6.0, ((0, 16), (1, 2))),
        "norm_gain": jnp.clip(1.0 + 0.18 * jax.random.normal(splits[4], (SECTIONS, WIDTH), jnp.float32), 0.1, 1.9),
        "query_weight": draw_query_weight(jax.random.fold_in(splits[9], 71), 0),
        "keyval_weight": draw_keyval_weight(jax.random.fold_in(splits[9], 71), 0),
        "output_weight": gaussian(splits[7], (SECTIONS, HEADS * HEAD_DIM, WIDTH), (HEADS * HEAD_DIM) ** -0.5, 0.09375, ((0, 16), (1, 2))),
        "evict_marks": draw_evict_marks(jax.random.fold_in(splits[9], 71), 0),
    }


EPSILON = 1e-05
NEG_LARGE = -1e+30

def root_norm(features, gain_row):
    values = features.astype(jnp.float32)
    factor = lax.rsqrt(lax.optimization_barrier(jnp.mean(values * values, axis=-1, keepdims=True)) + EPSILON)
    return values * factor * gain_row

def settle(values):
    return lax.optimization_barrier(values.astype(jnp.bfloat16))

def causal_probs(scores):
    length = scores.shape[-1]
    allowed = jnp.arange(length)[:, None] >= jnp.arange(length)[None, :]
    masked = jnp.where(allowed, scores, NEG_LARGE)
    row_max = lax.optimization_barrier(jnp.max(masked, axis=-1, keepdims=True))
    raised = jnp.exp(masked - row_max)
    return raised / lax.optimization_barrier(jnp.sum(raised, axis=-1, keepdims=True))

def one_section(current, back_rows, upstream, gain_row, query_weight, keyval_weight, output_weight):
    length = current.shape[0]
    group_size = HEADS // KV_HEADS
    head_scale = HEAD_DIM ** (-0.5)
    query_cols = HEADS * HEAD_DIM // N_TENSOR
    keyval_cols = KV_HEADS * HEAD_DIM // N_TENSOR
    keyval_flat = keyval_weight.reshape(WIDTH, 2 * KV_HEADS * HEAD_DIM)

    def project(normed):
        queries = settle(jnp.dot(normed, query_weight, preferred_element_type=jnp.float32))
        keyvals = settle(jnp.dot(normed, keyval_flat, preferred_element_type=jnp.float32))
        queries = queries.astype(jnp.float32).reshape(length, KV_HEADS, group_size, HEAD_DIM)
        keyvals = keyvals.astype(jnp.float32).reshape(length, 2, KV_HEADS, HEAD_DIM)
        return (queries, keyvals[:, 0], keyvals[:, 1])

    def scores_of(queries, key_rows):
        return causal_probs(jnp.einsum('tkgh,ukh->kgtu', queries, key_rows) * head_scale)
    normed_now = root_norm(current, gain_row).astype(jnp.bfloat16)
    normed_back = root_norm(back_rows, gain_row).astype(jnp.bfloat16)
    query_now, key_now, value_now = project(normed_now)
    probs_now = scores_of(query_now, key_now)
    weights_now = settle(probs_now).astype(jnp.float32)
    context_now = settle(jnp.einsum('kgtu,ukh->tkgh', weights_now, value_now)).astype(jnp.float32)
    context_groups = context_now.reshape(length, N_TENSOR, query_cols)
    out_groups = output_weight.astype(jnp.float32).reshape(N_TENSOR, query_cols, WIDTH)
    forward_parts = settle(jnp.einsum('tnc,ncd->ntd', context_groups, out_groups)).astype(jnp.float32)
    forward_sum = lax.optimization_barrier(jnp.sum(forward_parts, axis=0))
    updated = (current.astype(jnp.float32) + forward_sum).astype(jnp.bfloat16)
    query_back, key_back, value_back = project(normed_back)
    probs_back = scores_of(query_back, key_back)
    weights_back = settle(probs_back).astype(jnp.float32)
    grad_context = settle(jnp.einsum('td,cd->tc', upstream.astype(jnp.float32), output_weight.astype(jnp.float32)))
    grad_context = grad_context.astype(jnp.float32).reshape(length, KV_HEADS, group_size, HEAD_DIM)
    grad_value = settle(jnp.einsum('kgtu,tkgh->ukh', weights_back, grad_context)).astype(jnp.float32)
    grad_prob = jnp.einsum('tkgh,ukh->kgtu', grad_context, value_back)
    grad_score = probs_back * (grad_prob - lax.optimization_barrier(jnp.sum(probs_back * grad_prob, axis=-1, keepdims=True))) * head_scale
    grad_score = settle(grad_score).astype(jnp.float32)
    grad_query = settle(jnp.einsum('kgtu,ukh->tkgh', grad_score, key_back)).astype(jnp.float32)
    grad_key = settle(jnp.einsum('kgtu,tkgh->ukh', grad_score, query_back)).astype(jnp.float32)
    grad_keyval = jnp.stack([grad_key, grad_value], axis=1).reshape(length, 2, N_TENSOR, keyval_cols)
    query_groups = query_weight.astype(jnp.float32).reshape(WIDTH, N_TENSOR, query_cols)
    keyval_groups = keyval_weight.astype(jnp.float32).reshape(WIDTH, 2, N_TENSOR, keyval_cols)
    backward_parts = jnp.einsum('tnc,dnc->ntd', grad_query.reshape(length, N_TENSOR, query_cols), query_groups)
    backward_parts = backward_parts + jnp.einsum('tjnc,djnc->ntd', grad_keyval, keyval_groups)
    backward_sum = lax.optimization_barrier(jnp.sum(settle(backward_parts).astype(jnp.float32), axis=0))
    normed_out, pull_back = jax.vjp(lambda inputs: root_norm(inputs, gain_row), back_rows.astype(jnp.float32))
    norm_grad = pull_back(backward_sum)[0]
    passed = (upstream.astype(jnp.float32) + norm_grad).astype(jnp.bfloat16)
    return (updated, passed)

def reference(activations, upstream_grad, stash_blocks, guest_blocks, norm_gain, query_weight, keyval_weight, output_weight, evict_marks):
    row_count = TOK // N_TENSOR
    block_rows = row_count // BLOCKS
    token_marks = jnp.broadcast_to(evict_marks[:, None, :, None], (SECTIONS, N_TENSOR, BLOCKS, block_rows)).reshape(SECTIONS, TOK)
    moved = (token_marks == 1)[:, :, None]
    back_rows = jnp.where(moved, guest_blocks[::-1], stash_blocks)

    def run_section(inputs):
        return one_section(*inputs)
    updated, passed = lax.map(run_section, (activations, back_rows, upstream_grad, norm_gain, query_weight, keyval_weight, output_weight))
    zero_section = jnp.zeros_like(activations[:1])
    next_input = jnp.concatenate([zero_section, updated[:-1]], axis=0)
    prev_grad = jnp.concatenate([passed[1:], zero_section], axis=0)
    zero_all = jnp.zeros_like(activations)
    kept_stash = jnp.where(moved, zero_all, activations)
    held_blocks = jnp.where(moved, activations, zero_all)[::-1]
    return (next_input, prev_grad, kept_stash, held_blocks)
```

```python
import jax
import jax.numpy as jnp
from jax import lax
from jax.experimental import pallas as pl
from jax.experimental.pallas import tpu as pltpu
from jax.sharding import PartitionSpec as P

HEADS = 32
KV_HEADS = 8
HEAD_DIM = 128
GROUP = HEADS // KV_HEADS
MOST_EVICT = 8

EPSILON = 1e-05
NEG_LARGE = -1e30
SCALE = HEAD_DIM ** (-0.5)
ROW_STEP = 16
VMEM_BYTES = 56 * 1024 * 1024


def shifted(x, axis, by):
    peers = lax.axis_size(axis)
    pairs = [(i, i + by) for i in range(peers) if 0 <= i + by < peers]
    return lax.ppermute(x, axis, pairs)


def crossed(x, by):
    peers = lax.axis_size("section")
    pairs = [
        (i * 2 + j, (i + by) * 2 + 1 - j) for i in range(peers) if 0 <= i + by < peers for j in (0, 1)
    ]
    return lax.ppermute(x, ("section", "tensor"), pairs)


def mirrored(x):
    peers = lax.axis_size("section")
    return lax.ppermute(x, "section", [(i, peers - 1 - i) for i in range(peers)])


def swapped(x):
    return lax.ppermute(x, "tensor", [(0, 1), (1, 0)])


def nn(a, b):
    return lax.dot_general(a, b, (((1,), (0,)), ((), ())), preferred_element_type=jnp.float32)


def nt(a, b):
    return lax.dot_general(a, b, (((1,), (1,)), ((), ())), preferred_element_type=jnp.float32)


def tn(a, b):
    return lax.dot_general(a, b, (((0,), (0,)), ((), ())), preferred_element_type=jnp.float32)


def norm_rows(source, target, at, gain):
    @pl.loop(0, source.shape[0] // ROW_STEP)
    def _(step):
        start = pl.multiple_of(step * ROW_STEP, ROW_STEP)
        rows = source[pl.ds(start, ROW_STEP), :].astype(jnp.float32)
        factor = lax.rsqrt(jnp.mean(rows * rows, axis=-1, keepdims=True) + EPSILON)
        target[pl.ds(pl.multiple_of(at + start, ROW_STEP), ROW_STEP), :] = (
            rows * factor * gain
        ).astype(jnp.bfloat16)


def columns_of(left, weight, target, width):
    @pl.loop(0, weight.shape[1] // width)
    def _(step):
        at = pl.ds(pl.multiple_of(step * width, width), width)
        target[:, at] = nn(left[...], weight[:, at]).astype(target.dtype)


def causal_mask(first, length):
    def tokens(dim):
        place = lax.broadcasted_iota(jnp.int32, (length, length), dim) + first
        return jnp.where(place >= length, place - length, place)

    return tokens(0) >= tokens(1)


def causal_probs(queries, keys, allowed):
    scores = jnp.where(allowed, nt(queries, keys) * SCALE, NEG_LARGE)
    raised = jnp.exp(scores - jnp.max(scores, axis=-1, keepdims=True))
    return raised * (1.0 / jnp.sum(raised, axis=-1, keepdims=True))


def head_at(h):
    return slice(h * HEAD_DIM, (h + 1) * HEAD_DIM)


def forward_kernel(
    first_ref, own_ref, rest_ref, gain_ref, wq_ref, wkv_ref, wo_ref,
    own_out, rest_out, normed, total, query, keyval, context,
):
    group = pl.program_id(0)
    row_count = own_ref.shape[0]
    length, width = normed.shape

    @pl.when(group == 0)
    def _():
        norm_rows(own_ref, normed, 0, gain_ref[...])
        norm_rows(rest_ref, normed, row_count, gain_ref[...])

    columns_of(normed, wkv_ref, keyval, 2 * HEAD_DIM)
    columns_of(normed, wq_ref, query, 2 * HEAD_DIM)
    allowed = causal_mask(first_ref[0], length)
    keys, values = keyval[:, :HEAD_DIM], keyval[:, HEAD_DIM:]
    for h in range(GROUP):
        weights = causal_probs(query[:, head_at(h)], keys, allowed).astype(jnp.bfloat16)
        context[:, head_at(h)] = nn(weights, values).astype(jnp.bfloat16)

    step_width = 512

    @pl.loop(0, width // step_width)
    def _(step):
        at = pl.ds(pl.multiple_of(step * step_width, step_width), step_width)
        part = nn(context[...], wo_ref[:, at])

        @pl.when(group == 0)
        def _():
            total[:, at] = part

        @pl.when(group > 0)
        def _():
            total[:, at] += part

    @pl.when(group == pl.num_programs(0) - 1)
    def _():
        own_out[...] = (own_ref[...].astype(jnp.float32) + total[:row_count, :]).astype(jnp.bfloat16)
        rest_out[...] = total[row_count:, :].astype(jnp.bfloat16)


def backward_kernel(
    first_ref, own_ref, rest_ref, up_own_ref, up_rest_ref, gain_ref, wq_ref, wkv_ref, wo_ref,
    own_out, rest_out, normed, upstream, total, query, keyval, grad_context, grad_query, grad_keyval,
):
    group = pl.program_id(0)
    row_count = own_ref.shape[0]
    length, width = normed.shape

    @pl.when(group == 0)
    def _():
        norm_rows(own_ref, normed, 0, gain_ref[...])
        norm_rows(rest_ref, normed, row_count, gain_ref[...])
        upstream[:row_count, :] = up_own_ref[...]
        upstream[row_count:, :] = up_rest_ref[...]

    columns_of(normed, wkv_ref, keyval, 2 * HEAD_DIM)
    columns_of(normed, wq_ref, query, 2 * HEAD_DIM)

    @pl.loop(0, wo_ref.shape[0] // (2 * HEAD_DIM))
    def _(step):
        at = pl.ds(pl.multiple_of(step * 2 * HEAD_DIM, 2 * HEAD_DIM), 2 * HEAD_DIM)
        grad_context[:, at] = nt(upstream[...], wo_ref[at, :]).astype(jnp.bfloat16)

    allowed = causal_mask(first_ref[0], length)
    keys, values = keyval[:, :HEAD_DIM], keyval[:, HEAD_DIM:]
    grad_key = grad_value = None
    for h in range(GROUP):
        queries, grads = query[:, head_at(h)], grad_context[:, head_at(h)]
        probs = causal_probs(queries, keys, allowed)
        value_part = tn(probs.astype(jnp.bfloat16), grads)
        grad_prob = nt(grads, values)
        mean_grad = jnp.sum(probs * grad_prob, axis=-1, keepdims=True)
        grad_score = (probs * (grad_prob - mean_grad) * SCALE).astype(jnp.bfloat16)
        grad_query[:, head_at(h)] = nn(grad_score, keys).astype(jnp.bfloat16)
        key_part = tn(grad_score, queries)
        grad_key = key_part if h == 0 else grad_key + key_part
        grad_value = value_part if h == 0 else grad_value + value_part
    grad_keyval[:, :HEAD_DIM] = grad_key.astype(jnp.bfloat16)
    grad_keyval[:, HEAD_DIM:] = grad_value.astype(jnp.bfloat16)

    step_width = 512

    @pl.loop(0, width // step_width)
    def _(step):
        at = pl.ds(pl.multiple_of(step * step_width, step_width), step_width)
        part = nt(grad_query[...], wq_ref[at, :]) + nt(grad_keyval[...], wkv_ref[at, :])

        @pl.when(group == 0)
        def _():
            total[:, at] = part

        @pl.when(group > 0)
        def _():
            total[:, at] += part

    @pl.when(group == pl.num_programs(0) - 1)
    def _():
        gain = gain_ref[...]

        def norm_grad(rows, grads):
            factor = lax.rsqrt(jnp.mean(rows * rows, axis=-1, keepdims=True) + EPSILON)
            grads = grads * gain
            mean = jnp.mean(rows * grads, axis=-1, keepdims=True)
            return grads * factor - rows * (factor * factor * factor * mean)

        @pl.loop(0, row_count // ROW_STEP)
        def _(step):
            at = pl.ds(pl.multiple_of(step * ROW_STEP, ROW_STEP), ROW_STEP)
            grads = norm_grad(own_ref[at, :].astype(jnp.float32), total[at, :])
            own_out[at, :] = (up_own_ref[at, :].astype(jnp.float32) + grads).astype(jnp.bfloat16)

        @pl.loop(0, (length - row_count) // ROW_STEP)
        def _(step):
            start = pl.multiple_of(step * ROW_STEP, ROW_STEP)
            at = pl.ds(start, ROW_STEP)
            among = pl.ds(pl.multiple_of(row_count + start, ROW_STEP), ROW_STEP)
            grads = norm_grad(rest_ref[at, :].astype(jnp.float32), total[among, :])
            rest_out[at, :] = grads.astype(jnp.bfloat16)


def layer_call(kernel, first, row_arrays, gain, weights, scratch, flops, name):
    query_weight, keyval_weight, output_weight = weights
    width = query_weight.shape[0]
    groups = keyval_weight.shape[1] // (2 * HEAD_DIM)
    own, rest = row_arrays[:2]
    whole = lambda shape: pl.BlockSpec(shape, lambda g: (0, 0))
    read = sum(x.size for x in (*row_arrays, *weights)) * 2
    return pl.pallas_call(
        kernel,
        grid=(groups,),
        in_specs=[
            pl.BlockSpec(memory_space=pltpu.SMEM),
            *(whole(x.shape) for x in row_arrays),
            whole(gain.shape),
            pl.BlockSpec((width, GROUP * HEAD_DIM), lambda g: (0, g)),
            pl.BlockSpec((width, 2 * HEAD_DIM), lambda g: (0, g)),
            pl.BlockSpec((GROUP * HEAD_DIM, width), lambda g: (g, 0)),
        ],
        out_specs=[whole(own.shape), whole(rest.shape)],
        out_shape=[
            jax.ShapeDtypeStruct(own.shape, jnp.bfloat16),
            jax.ShapeDtypeStruct(rest.shape, jnp.bfloat16),
        ],
        scratch_shapes=scratch,
        compiler_params=pltpu.CompilerParams(vmem_limit_bytes=VMEM_BYTES),
        cost_estimate=pl.CostEstimate(flops=flops, bytes_accessed=read, transcendentals=0),
        name=name,
    )(first, *row_arrays, gain, *weights)


def forward_layer(first, own, rest, gain, weights):
    length, width = own.shape[0] + rest.shape[0], own.shape[1]
    cols = GROUP * HEAD_DIM
    scratch = [
        pltpu.VMEM((length, width), jnp.bfloat16),
        pltpu.VMEM((length, width), jnp.float32),
        pltpu.VMEM((length, cols), jnp.bfloat16),
        pltpu.VMEM((length, 2 * HEAD_DIM), jnp.bfloat16),
        pltpu.VMEM((length, cols), jnp.bfloat16),
    ]
    flops = 2 * length * sum(x.size for x in weights)
    return layer_call(forward_kernel, first, (own, rest), gain, weights, scratch, flops, "forward_layer")


def backward_layer(first, own, rest, up_own, up_rest, gain, weights):
    length, width = own.shape[0] + rest.shape[0], own.shape[1]
    cols = GROUP * HEAD_DIM
    scratch = [
        pltpu.VMEM((length, width), jnp.bfloat16),
        pltpu.VMEM((length, width), jnp.bfloat16),
        pltpu.VMEM((length, width), jnp.float32),
        pltpu.VMEM((length, cols), jnp.bfloat16),
        pltpu.VMEM((length, 2 * HEAD_DIM), jnp.bfloat16),
        pltpu.VMEM((length, cols), jnp.bfloat16),
        pltpu.VMEM((length, cols), jnp.bfloat16),
        pltpu.VMEM((length, 2 * HEAD_DIM), jnp.bfloat16),
    ]
    flops = 2 * length * (sum(x.size for x in weights) + weights[0].size + weights[1].size)
    rows = (own, rest, up_own, up_rest)
    return layer_call(backward_kernel, first, rows, gain, weights, scratch, flops, "backward_layer")


def packing(marks, row_count):
    block_rows = row_count // marks.shape[0]
    rank = jnp.cumsum(marks) - 1
    place = jnp.repeat(rank, block_rows) * block_rows + jnp.arange(row_count) % block_rows
    chosen = jnp.repeat(marks, block_rows) == 1
    place = jnp.where(chosen, place, -1)
    slots = jnp.arange(MOST_EVICT * block_rows)
    return (place[None, :] == slots[:, None]).astype(jnp.bfloat16), chosen[:, None]


def others_rows(x):
    if lax.axis_size("tensor") == 2:
        return swapped(x)
    row_count = x.shape[0]
    rows = lax.all_gather(x, "tensor", axis=0, tiled=True)
    return jnp.roll(rows, -row_count * lax.axis_index("tensor"), axis=0)[row_count:]


def summed_and_moved(own, rest, by):
    if lax.axis_size("tensor") == 2:
        base, term = shifted(own, "section", by), crossed(rest, by)
        return (base.astype(jnp.float32) + term.astype(jnp.float32)).astype(jnp.bfloat16)
    rows = jnp.concatenate([own, rest], axis=0).astype(jnp.float32)
    rows = jnp.roll(rows, own.shape[0] * lax.axis_index("tensor"), axis=0)
    rows = lax.psum_scatter(rows, "tensor", scatter_dimension=0, tiled=True)
    return shifted(rows.astype(jnp.bfloat16), "section", by)


def local(
    activations,
    upstream_grad,
    stash_blocks,
    guest_blocks,
    norm_gain,
    query_weight,
    keyval_weight,
    output_weight,
    evict_marks,
):
    sections = lax.axis_size("section")
    section_index = lax.axis_index("section")
    current = activations[0]
    upstream = upstream_grad[0]
    stash_rows = stash_blocks[0]
    guest_rows = guest_blocks[0]
    row_count, model_width = current.shape
    current_rest = others_rows(current)
    upstream_rest = others_rows(upstream)

    own_marks = lax.dynamic_index_in_dim(evict_marks, section_index, 0, keepdims=False)
    mirror_marks = lax.dynamic_index_in_dim(
        evict_marks, sections - 1 - section_index, 0, keepdims=False
    )
    pack_own, own_mask = packing(own_marks, row_count)
    pack_mirror, _ = packing(mirror_marks, row_count)
    guests_back = mirrored(nn(pack_mirror, guest_rows).astype(jnp.bfloat16))
    arrived = mirrored(nn(pack_own, current).astype(jnp.bfloat16))
    back_rows = jnp.where(own_mask, tn(pack_own, guests_back).astype(jnp.bfloat16), stash_rows)
    back_rest = others_rows(back_rows)
    held_rows = tn(pack_mirror, arrived).astype(jnp.bfloat16)
    kept_rows = jnp.where(own_mask, jnp.zeros_like(current), current)

    first = (lax.axis_index("tensor") * row_count).astype(jnp.int32)[None]
    keyval_cols = keyval_weight.shape[3]
    keyval_flat = keyval_weight[0].reshape(model_width, 2, keyval_cols // HEAD_DIM, HEAD_DIM)
    keyval_flat = keyval_flat.transpose(0, 2, 1, 3).reshape(model_width, 2 * keyval_cols)
    weights = (query_weight[0], keyval_flat, output_weight[0])

    ahead_own, ahead_rest = forward_layer(first, current, current_rest, norm_gain, weights)
    next_input = summed_and_moved(ahead_own, ahead_rest, 1)
    grad_own, grad_rest = backward_layer(
        first, back_rows, back_rest, upstream, upstream_rest, norm_gain, weights
    )
    prev_grad = summed_and_moved(grad_own, grad_rest, -1)
    return (next_input[None], prev_grad[None], kept_rows[None], held_rows[None])


def solution(mesh):
    rows = P("section", "tensor", None)
    placed = (
        rows,
        rows,
        rows,
        rows,
        P("section", None),
        P("section", None, "tensor"),
        P("section", None, None, "tensor"),
        P("section", "tensor", None),
        P(),
    )
    return jax.shard_map(
        local, mesh=mesh, in_specs=placed, out_specs=(rows, rows, rows, rows), check_vma=False
    )
```

```python
import jax
import jax.numpy as jnp
from jax import lax
from jax.experimental import pallas as pl
from jax.experimental.pallas import tpu as pltpu
from jax.sharding import PartitionSpec as P

HEADS = 32
KV_HEADS = 8
HEAD_DIM = 128
GROUP = HEADS // KV_HEADS
MOST_EVICT = 8

EPSILON = 1e-05
NEG_LARGE = -1e30
SCALE = HEAD_DIM ** (-0.5)
ROW_STEP = 16
VMEM_BYTES = 16 * 1024 * 1024
SLOTS = 2


def shifted(x, axis, by):
    peers = lax.axis_size(axis)
    pairs = [(i, i + by) for i in range(peers) if 0 <= i + by < peers]
    return lax.ppermute(x, axis, pairs)


def crossed(x, by):
    peers = lax.axis_size("section")
    pairs = [
        (i * 2 + j, (i + by) * 2 + 1 - j) for i in range(peers) if 0 <= i + by < peers for j in (0, 1)
    ]
    return lax.ppermute(x, ("section", "tensor"), pairs)


def mirrored(x):
    peers = lax.axis_size("section")
    return lax.ppermute(x, "section", [(i, peers - 1 - i) for i in range(peers)])


def swapped(x):
    return lax.ppermute(x, "tensor", [(0, 1), (1, 0)])


def nn(a, b):
    return lax.dot_general(a, b, (((1,), (0,)), ((), ())), preferred_element_type=jnp.float32)


def nt(a, b):
    return lax.dot_general(a, b, (((1,), (1,)), ((), ())), preferred_element_type=jnp.float32)


def tn(a, b):
    return lax.dot_general(a, b, (((0,), (0,)), ((), ())), preferred_element_type=jnp.float32)


ANY = pl.BlockSpec(memory_space=pl.ANY)
KEYVAL = 2 * HEAD_DIM
COLS = GROUP * HEAD_DIM


def part(g, width):
    return slice(g * width, (g + 1) * width)


def call(kernel, inputs, outputs, scratch, flops, after=(), specs=None):
    near = pl.BlockSpec(memory_space=pltpu.VMEM)
    read = sum(x.size * x.dtype.itemsize for x in inputs)

    def body(*refs):
        kernel(*refs[: len(inputs)], *refs[len(inputs) + len(after) :])

    return pl.pallas_call(
        body,
        in_specs=[*(specs or [near] * len(inputs)), *([ANY] * len(after))],
        out_specs=[near] * len(outputs),
        out_shape=[
            jax.ShapeDtypeStruct(x, jnp.bfloat16) if isinstance(x, tuple) else x for x in outputs
        ],
        scratch_shapes=scratch,
        compiler_params=pltpu.CompilerParams(vmem_limit_bytes=VMEM_BYTES),
        cost_estimate=pl.CostEstimate(flops=flops, bytes_accessed=read, transcendentals=0),
        name=kernel.__name__,
    )(*inputs, *after)


def norm_rows(source, target, gain):
    @pl.loop(0, source.shape[0] // ROW_STEP, unroll=2)
    def _(step):
        at = pl.ds(pl.multiple_of(step * ROW_STEP, ROW_STEP), ROW_STEP)
        rows = source[at, :].astype(jnp.float32)
        factor = lax.rsqrt(jnp.mean(rows * rows, axis=-1, keepdims=True) + EPSILON)
        target[at, :] = (rows * factor * gain).astype(jnp.bfloat16)


def pack_and_copy(pack, chosen, rows, copied, kept, packed):
    copied[...] = rows[...]
    kept[...] = jnp.where(chosen[...] == 1, jnp.zeros_like(rows), rows[...])
    packed[...] = nn(pack[...], rows[...]).astype(jnp.bfloat16)


def pack_rows(pack, rows, out):
    out[...] = nn(pack[...], rows[...]).astype(jnp.bfloat16)


def unpack_rows(pack, chosen, rows, other, out):
    placed = tn(pack[...], rows[...]).astype(jnp.bfloat16)
    out[...] = jnp.where(chosen[...] == 1, placed, other[...])


def copy_rows(pairs, sems):
    copies = [pltpu.make_async_copy(far, near, sems.at[i]) for i, (far, near) in enumerate(pairs)]
    for copy in copies:
        copy.start()
    return copies


def streamed(pairs, sems):
    copies = [pltpu.make_async_copy(far, near, sems.at[i]) for i, (far, near) in enumerate(pairs)]
    for copy in copies[:SLOTS]:
        copy.start()
    return copies


def held(x):
    return pltpu.with_memory_space_constraint(x, pltpu.VMEM)


def far(x):
    return pltpu.with_memory_space_constraint(x, pltpu.HBM)


HELD_WIDTH = 1024


def load_weights(wq_far, wkv_far, *refs):
    *wq, wkv, done, sems = refs
    width = wq[0].shape[1]
    pairs = [(wq_far.at[:, part(i, width)], near) for i, near in enumerate(wq)]
    for copy in copy_rows([(wkv_far, wkv), *pairs], sems):
        copy.wait()
    done[...] = jnp.zeros_like(done)


def loaded(wq, wkv, after):
    count = max(1, wq.shape[1] // HELD_WIDTH)
    wq_part = pltpu.VMEM((wq.shape[0], wq.shape[1] // count), wq.dtype)
    outputs = [wq_part] * count + [pltpu.VMEM(wkv.shape, wkv.dtype), (16, HEAD_DIM)]
    scratch = [pltpu.SemaphoreType.DMA((count + 1,))]
    return call(load_weights, (far(wq), far(wkv)), outputs, scratch, 0, after, [ANY] * 2)


def project(normed, weights, query, keyval, start):
    *wq, wkv = weights
    keyval[start:, :] = nn(normed[...], wkv[...]).astype(jnp.bfloat16)
    for i, weight in enumerate(wq):
        query[start:, part(i, weight.shape[1])] = nn(normed[...], weight[...]).astype(jnp.bfloat16)


def own_projection(rows, gain, *refs):
    *weights, query, keyval, normed = refs
    norm_rows(rows, normed, gain[...])
    project(normed, weights, query, keyval, 0)


def columns(weights):
    return sum(x.shape[1] for x in weights)


def project_own(rows, gain, weights, after):
    outputs = [(rows.shape[0], columns(weights[:-1])), (rows.shape[0], columns(weights[-1:]))]
    flops = 2 * rows.size * columns(weights)
    inputs = (rows, gain, *(held(x) for x in weights))
    return call(own_projection, inputs, outputs, [bf16(*rows.shape)], flops, after)


def context_gradient(own, rest, wo_far, out, upstream, wo, sems, row_sems):
    row_count, groups = own.shape[0], out.shape[1] // COLS
    pairs = [(own, upstream.at[:row_count, :]), (rest, upstream.at[row_count:, :])]
    rows = copy_rows(pairs, row_sems)
    copies = streamed([(wo_far.at[part(g, COLS), :], wo.at[g % SLOTS]) for g in range(groups)], sems)
    for copy in rows:
        copy.wait()
    for g in range(groups):
        copies[g].wait()
        out[:, part(g, COLS)] = nt(upstream[...], wo[g % SLOTS]).astype(jnp.bfloat16)
        if g + SLOTS < groups:
            copies[g + SLOTS].start()


def grad_context_of(own, rest, wo, after):
    length = own.shape[0] + rest.shape[0]
    dma = pltpu.SemaphoreType.DMA
    slots = bf16(SLOTS, COLS, own.shape[1])
    scratch = [bf16(length, own.shape[1]), slots, dma((wo.shape[0] // COLS,)), dma((2,))]
    flops = 2 * length * wo.size
    outputs = [(length, wo.shape[0])]
    return call(context_gradient, (own, rest, far(wo)), outputs, scratch, flops, after, [ANY] * 3)[0]


def token_numbers(first, length, dim):
    place = lax.broadcasted_iota(jnp.int32, (length, length), dim) + first
    return jnp.where(place >= length, place - length, place)


def causal_bias(first, length):
    allowed = token_numbers(first, length, 1) >= token_numbers(first, length, 0)
    return jnp.where(allowed, 0.0, NEG_LARGE)


def stacked(ref, g):
    return jnp.concatenate([ref[:, part(h, HEAD_DIM)] for h in range(g * GROUP, (g + 1) * GROUP)], axis=0)


def causal_probs(keys, queries, bias):
    scores = nt(keys, queries) * SCALE + jnp.concatenate([bias[...]] * GROUP, axis=1)
    raised = jnp.exp(scores - jnp.max(scores, axis=0, keepdims=True))
    return raised * (1.0 / jnp.sum(raised, axis=0, keepdims=True))


def forward_layer(
    own, rest, gain, query_own, keyval_own, wo_far, *refs
):
    own_out, rest_out, wo, normed, query, keyval, context, bias, sems, out_sems = refs[-10:]
    weights = refs[:-10]
    row_count, width = own.shape
    length = row_count + rest.shape[0]
    groups = keyval.shape[1] // KEYVAL
    step_width = 1024
    rows = copy_rows([(query_own, query.at[:row_count, :]), (keyval_own, keyval.at[:row_count, :])], sems)
    parts = [part(step, step_width) for step in range(width // step_width)]
    out_copies = streamed([(wo_far.at[:, at], wo.at[i % SLOTS]) for i, at in enumerate(parts)], out_sems)
    norm_rows(rest, normed, gain[...])
    bias[...] = causal_bias(lax.axis_index("tensor") * row_count, length)
    project(normed, weights, query, keyval, row_count)
    for copy in rows:
        copy.wait()
    for g in range(groups):
        keys, values = keyval[:, part(g, HEAD_DIM)], keyval[:, part(groups + g, HEAD_DIM)]
        weights = causal_probs(keys, stacked(query, g), bias).astype(jnp.bfloat16)
        found = tn(weights, values).astype(jnp.bfloat16)
        for h in range(GROUP):
            context[:, part(g * GROUP + h, HEAD_DIM)] = found[part(h, length), :]
    for i, at in enumerate(parts):
        out_copies[i].wait()
        term = nn(context[...], wo[i % SLOTS])
        own_out[:, at] = (own[:, at].astype(jnp.float32) + term[:row_count]).astype(jnp.bfloat16)
        rest_out[:, at] = term[row_count:].astype(jnp.bfloat16)
        if i + SLOTS < len(parts):
            out_copies[i + SLOTS].start()


def backward_layer(
    own, rest, up_own, gain, query_own, keyval_own, grad_context, *refs
):
    own_out, rest_out, normed, query, keyval, grad_query, grad_keyval = refs[-12:-5]
    total, squares, products, bias, sems = refs[-5:]
    *wq, wkv = weights = refs[:-12]
    row_count, width = own.shape
    length = row_count + rest.shape[0]
    groups = keyval.shape[1] // KEYVAL
    rows = copy_rows([(query_own, query.at[:row_count, :]), (keyval_own, keyval.at[:row_count, :])], sems)
    norm_rows(rest, normed, gain[...])
    bias[...] = causal_bias(lax.axis_index("tensor") * row_count, length)
    project(normed, weights, query, keyval, row_count)
    for copy in rows:
        copy.wait()
    for g in range(groups):
        keys, values = keyval[:, part(g, HEAD_DIM)], keyval[:, part(groups + g, HEAD_DIM)]
        queries, above = stacked(query, g), stacked(grad_context, g)
        probs = causal_probs(keys, queries, bias)
        grad_value = nn(probs.astype(jnp.bfloat16), above)
        grad_prob = nt(values, above)
        mean_grad = jnp.sum(probs * grad_prob, axis=0, keepdims=True)
        grad_score = (probs * (grad_prob - mean_grad) * SCALE).astype(jnp.bfloat16)
        found = tn(grad_score, keys).astype(jnp.bfloat16)
        for h in range(GROUP):
            grad_query[:, part(g * GROUP + h, HEAD_DIM)] = found[part(h, length), :]
        grad_keyval[:, part(g, HEAD_DIM)] = nn(grad_score, queries).astype(jnp.bfloat16)
        grad_keyval[:, part(groups + g, HEAD_DIM)] = grad_value.astype(jnp.bfloat16)

    step_width = 512
    squares[...] = jnp.zeros_like(squares)
    products[...] = jnp.zeros_like(products)
    halves = ((own, 0, row_count), (rest, row_count, length))
    for step in range(width // step_width):
        at = part(step, step_width)
        term = nt(grad_keyval[...], wkv[at, :])
        for i, weight in enumerate(wq):
            term += nt(grad_query[:, part(i, weight.shape[1])], weight[at, :])
        term *= gain[:, at]
        total[:, at] = term
        for rows, start, stop in halves:
            values = rows[:, at].astype(jnp.float32)
            square, product = values * values, values * term[start:stop]
            lanes = [part(i, HEAD_DIM) for i in range(step_width // HEAD_DIM)]
            squares[start:stop, :] += sum(square[:, i] for i in lanes)
            products[start:stop, :] += sum(product[:, i] for i in lanes)

    def norm_grad(rows, at, among):
        factor = lax.rsqrt(jnp.sum(squares[among, :], axis=-1, keepdims=True) / width + EPSILON)
        mean = jnp.sum(products[among, :], axis=-1, keepdims=True) / width
        values = rows[at, :].astype(jnp.float32)
        return total[among, :] * factor - values * (factor * factor * factor * mean)

    @pl.loop(0, rest.shape[0] // ROW_STEP, unroll=2)
    def _(step):
        at = pl.ds(pl.multiple_of(step * ROW_STEP, ROW_STEP), ROW_STEP)
        among = pl.ds(pl.multiple_of(row_count + step * ROW_STEP, ROW_STEP), ROW_STEP)
        rest_out[at, :] = norm_grad(rest, at, among).astype(jnp.bfloat16)

    @pl.loop(0, row_count // ROW_STEP, unroll=2)
    def _(step):
        at = pl.ds(pl.multiple_of(step * ROW_STEP, ROW_STEP), ROW_STEP)
        own_out[at, :] = (up_own[at, :].astype(jnp.float32) + norm_grad(own, at, at)).astype(jnp.bfloat16)


def bf16(*shape):
    return pltpu.VMEM(shape, jnp.bfloat16)


def f32(*shape):
    return pltpu.VMEM(shape, jnp.float32)


def forward(own, rest, gain, projected, wo, weights, after):
    length, width = own.shape[0] + rest.shape[0], own.shape[1]
    queries, keyvals = (bf16(length, x.shape[1]) for x in projected)
    scratch = [
        bf16(SLOTS, wo.shape[0], 1024), bf16(*rest.shape), queries, keyvals, queries,
        f32(length, length), pltpu.SemaphoreType.DMA((2,)), pltpu.SemaphoreType.DMA((width // 1024,)),
    ]
    near = pl.BlockSpec(memory_space=pltpu.VMEM)
    specs = [near, near, near, ANY, ANY, ANY, *([near] * len(weights))]
    flops = 2 * rest.size * columns(weights) + 2 * length * wo.size
    inputs = (own, rest, gain, *projected, far(wo), *(held(x) for x in weights))
    return call(forward_layer, inputs, (own.shape, rest.shape), scratch, flops, after, specs)


def backward(own, rest, up_own, gain, projected, grad_context, weights, after):
    length, width = own.shape[0] + rest.shape[0], own.shape[1]
    queries, keyvals = (bf16(length, x.shape[1]) for x in projected)
    scratch = [
        bf16(*rest.shape), queries, keyvals, queries, keyvals,
        f32(length, width), f32(length, HEAD_DIM), f32(length, HEAD_DIM), f32(length, length),
        pltpu.SemaphoreType.DMA((2,)),
    ]
    near = pl.BlockSpec(memory_space=pltpu.VMEM)
    specs = [*([near] * 4), ANY, ANY, near, *([near] * len(weights))]
    flops = 2 * (rest.shape[0] + length) * width * columns(weights)
    inputs = (own, rest, up_own, gain, *projected, grad_context, *(held(x) for x in weights))
    return call(backward_layer, inputs, (own.shape, rest.shape), scratch, flops, after, specs)


def packing(marks, row_count):
    block_rows = row_count // marks.shape[0]
    rank = jnp.cumsum(marks) - 1
    place = jnp.repeat(rank, block_rows) * block_rows + jnp.arange(row_count) % block_rows
    chosen = jnp.repeat(marks, block_rows) == 1
    place = jnp.where(chosen, place, -1)
    slots = jnp.arange(MOST_EVICT * block_rows)
    return (place[None, :] == slots[:, None]).astype(jnp.bfloat16), chosen[:, None]


def others_rows(x):
    if lax.axis_size("tensor") == 2:
        return swapped(x)
    row_count = x.shape[0]
    rows = lax.all_gather(x, "tensor", axis=0, tiled=True)
    return jnp.roll(rows, -row_count * lax.axis_index("tensor"), axis=0)[row_count:]


def summed_and_moved(own, rest, by):
    if lax.axis_size("tensor") == 2:
        base, term = shifted(own, "section", by), crossed(rest, by)
        return (base.astype(jnp.float32) + term.astype(jnp.float32)).astype(jnp.bfloat16)
    rows = jnp.concatenate([own, rest], axis=0).astype(jnp.float32)
    rows = jnp.roll(rows, own.shape[0] * lax.axis_index("tensor"), axis=0)
    rows = lax.psum_scatter(rows, "tensor", scatter_dimension=0, tiled=True)
    return shifted(rows.astype(jnp.bfloat16), "section", by)


def local(
    activations,
    upstream_grad,
    stash_blocks,
    guest_blocks,
    norm_gain,
    query_weight,
    keyval_weight,
    output_weight,
    evict_marks,
):
    sections = lax.axis_size("section")
    section_index = lax.axis_index("section")
    current = activations[0]
    upstream = upstream_grad[0]
    stash_rows = stash_blocks[0]
    guest_rows = guest_blocks[0]
    row_count, model_width = current.shape
    upstream_rest = others_rows(upstream)

    own_marks = lax.dynamic_index_in_dim(evict_marks, section_index, 0, keepdims=False)
    mirror_marks = lax.dynamic_index_in_dim(
        evict_marks, sections - 1 - section_index, 0, keepdims=False
    )
    pack_own, own_mask = packing(own_marks, row_count)
    pack_mirror, _ = packing(mirror_marks, row_count)
    packed_shape = (pack_own.shape[0], model_width)
    pack_flops = 2 * pack_own.size * model_width
    guests = call(pack_rows, (pack_mirror, guest_rows), [packed_shape], [], pack_flops)[0]
    guests_back = mirrored(guests)
    chosen = own_mask.astype(jnp.int32)
    shapes = [current.shape, current.shape, packed_shape]
    current_copy, kept_rows, leaving = call(
        pack_and_copy, (pack_own, chosen, current), shapes, [], pack_flops, (guests,)
    )
    current_rest = others_rows(current_copy)
    arrived = mirrored(leaving)

    keyval_cols = keyval_weight.shape[3]
    keyval_flat = keyval_weight[0].reshape(model_width, 2 * keyval_cols)
    *weights, done = loaded(query_weight[0], keyval_flat, (current_copy,))
    wo = output_weight[0]

    grad_context = grad_context_of(upstream, upstream_rest, wo, (done,))
    unpack_inputs = (pack_own, chosen, guests_back, stash_rows)
    back_rows = call(
        unpack_rows, unpack_inputs, [current.shape], [], pack_flops, (grad_context,)
    )[0]
    back_rest = others_rows(back_rows)
    held_rows = tn(pack_mirror, arrived).astype(jnp.bfloat16)
    ahead = project_own(current, norm_gain, weights, (back_rows,))
    behind = project_own(back_rows, norm_gain, weights, ahead)

    ahead_own, ahead_rest = forward(current, current_rest, norm_gain, ahead, wo, weights, (*behind, arrived))
    next_input = summed_and_moved(ahead_own, ahead_rest, 1)
    grad_own, grad_rest = backward(
        back_rows, back_rest, upstream, norm_gain, behind, grad_context, weights, (ahead_rest,)
    )
    prev_grad = summed_and_moved(grad_own, grad_rest, -1)
    return (next_input[None], prev_grad[None], kept_rows[None], held_rows[None])


def solution(mesh):
    rows = P("section", "tensor", None)
    placed = (
        rows,
        rows,
        rows,
        rows,
        P("section", None),
        P("section", None, "tensor"),
        P("section", None, None, "tensor"),
        P("section", "tensor", None),
        P(),
    )
    return jax.shard_map(
        local, mesh=mesh, in_specs=placed, out_specs=(rows, rows, rows, rows), check_vma=False
    )
```

```python
import jax
import jax.numpy as jnp
from jax import lax
from jax.experimental import pallas as pl
from jax.experimental.pallas import tpu as pltpu
from jax.sharding import PartitionSpec as P

HEADS = 32
KV_HEADS = 8
HEAD_DIM = 128
GROUP = HEADS // KV_HEADS
MOST_EVICT = 8

EPSILON = 1e-05
NEG_LARGE = -1e30
SCALE = HEAD_DIM ** (-0.5)
ROW_STEP = 16
VMEM_BYTES = 16 * 1024 * 1024
SLOTS = 2


def shifted(x, axis, by):
    peers = lax.axis_size(axis)
    pairs = [(i, i + by) for i in range(peers) if 0 <= i + by < peers]
    return lax.ppermute(x, axis, pairs)


def crossed(x, by):
    peers = lax.axis_size("section")
    pairs = [
        (i * 2 + j, (i + by) * 2 + 1 - j) for i in range(peers) if 0 <= i + by < peers for j in (0, 1)
    ]
    return lax.ppermute(x, ("section", "tensor"), pairs)


def mirrored(x):
    peers = lax.axis_size("section")
    return lax.ppermute(x, "section", [(i, peers - 1 - i) for i in range(peers)])


def swapped(x):
    return lax.ppermute(x, "tensor", [(0, 1), (1, 0)])


def nn(a, b):
    return lax.dot_general(a, b, (((1,), (0,)), ((), ())), preferred_element_type=jnp.float32)


def nt(a, b):
    return lax.dot_general(a, b, (((1,), (1,)), ((), ())), preferred_element_type=jnp.float32)


def tn(a, b):
    return lax.dot_general(a, b, (((0,), (0,)), ((), ())), preferred_element_type=jnp.float32)


ANY = pl.BlockSpec(memory_space=pl.ANY)
KEYVAL = 2 * HEAD_DIM
COLS = GROUP * HEAD_DIM


def part(g, width):
    return slice(g * width, (g + 1) * width)


def call(kernel, inputs, outputs, scratch, flops, after=(), specs=None):
    near = pl.BlockSpec(memory_space=pltpu.VMEM)
    read = sum(x.size * x.dtype.itemsize for x in inputs)

    def body(*refs):
        kernel(*refs[: len(inputs)], *refs[len(inputs) + len(after) :])

    return pl.pallas_call(
        body,
        in_specs=[*(specs or [near] * len(inputs)), *([ANY] * len(after))],
        out_specs=[near] * len(outputs),
        out_shape=[
            jax.ShapeDtypeStruct(x, jnp.bfloat16) if isinstance(x, tuple) else x for x in outputs
        ],
        scratch_shapes=scratch,
        compiler_params=pltpu.CompilerParams(vmem_limit_bytes=VMEM_BYTES),
        cost_estimate=pl.CostEstimate(flops=flops, bytes_accessed=read, transcendentals=0),
        name=kernel.__name__,
    )(*inputs, *after)


def norm_rows(source, target, gain):
    @pl.loop(0, source.shape[0] // ROW_STEP, unroll=2)
    def _(step):
        at = pl.ds(pl.multiple_of(step * ROW_STEP, ROW_STEP), ROW_STEP)
        rows = source[at, :].astype(jnp.float32)
        factor = lax.rsqrt(jnp.mean(rows * rows, axis=-1, keepdims=True) + EPSILON)
        target[at, :] = (rows * factor * gain).astype(jnp.bfloat16)


def pack_and_copy(pack, chosen, rows, copied, kept, packed):
    copied[...] = rows[...]
    kept[...] = jnp.where(chosen[...] == 1, jnp.zeros_like(rows), rows[...])
    packed[...] = nn(pack[...], rows[...]).astype(jnp.bfloat16)


def pack_rows(pack, rows, out):
    out[...] = nn(pack[...], rows[...]).astype(jnp.bfloat16)


def unpack_rows(pack, chosen, rows, other, out):
    placed = tn(pack[...], rows[...]).astype(jnp.bfloat16)
    out[...] = jnp.where(chosen[...] == 1, placed, other[...])


def copy_rows(pairs, sems):
    copies = [pltpu.make_async_copy(far, near, sems.at[i]) for i, (far, near) in enumerate(pairs)]
    for copy in copies:
        copy.start()
    return copies


def streamed(pairs, sems):
    copies = [pltpu.make_async_copy(far, near, sems.at[i]) for i, (far, near) in enumerate(pairs)]
    for copy in copies[:SLOTS]:
        copy.start()
    return copies


def held(x):
    return pltpu.with_memory_space_constraint(x, pltpu.VMEM)


def far(x):
    return pltpu.with_memory_space_constraint(x, pltpu.HBM)


HELD_WIDTH = 1024


def load_weights(wq_far, wkv_far, *refs):
    *wq, wkv, done, sems = refs
    width = wq[0].shape[1]
    pairs = [(wq_far.at[:, part(i, width)], near) for i, near in enumerate(wq)]
    for copy in copy_rows([(wkv_far, wkv), *pairs], sems):
        copy.wait()
    done[...] = jnp.zeros_like(done)


def loaded(wq, wkv, after):
    count = max(1, wq.shape[1] // HELD_WIDTH)
    wq_part = pltpu.VMEM((wq.shape[0], wq.shape[1] // count), wq.dtype)
    outputs = [wq_part] * count + [pltpu.VMEM(wkv.shape, wkv.dtype), (16, HEAD_DIM)]
    scratch = [pltpu.SemaphoreType.DMA((count + 1,))]
    return call(load_weights, (far(wq), far(wkv)), outputs, scratch, 0, after, [ANY] * 2)


def project(normed, weights, query, keyval, start):
    *wq, wkv = weights
    keyval[start:, :] = nn(normed[...], wkv[...]).astype(jnp.bfloat16)
    for i, weight in enumerate(wq):
        query[start:, part(i, weight.shape[1])] = nn(normed[...], weight[...]).astype(jnp.bfloat16)


def own_projection(rows, gain, *refs):
    *weights, query, keyval, normed = refs
    norm_rows(rows, normed, gain[...])
    project(normed, weights, query, keyval, 0)


def columns(weights):
    return sum(x.shape[1] for x in weights)


def project_own(rows, gain, weights, after):
    outputs = [(rows.shape[0], columns(weights[:-1])), (rows.shape[0], columns(weights[-1:]))]
    flops = 2 * rows.size * columns(weights)
    inputs = (rows, gain, *(held(x) for x in weights))
    return call(own_projection, inputs, outputs, [bf16(*rows.shape)], flops, after)


def context_gradient(own, rest, wo_far, out, upstream, wo, sems, row_sems):
    row_count, groups = own.shape[0], out.shape[1] // COLS
    pairs = [(own, upstream.at[:row_count, :]), (rest, upstream.at[row_count:, :])]
    rows = copy_rows(pairs, row_sems)
    copies = streamed([(wo_far.at[part(g, COLS), :], wo.at[g % SLOTS]) for g in range(groups)], sems)
    for copy in rows:
        copy.wait()
    for g in range(groups):
        copies[g].wait()
        out[:, part(g, COLS)] = nt(upstream[...], wo[g % SLOTS]).astype(jnp.bfloat16)
        if g + SLOTS < groups:
            copies[g + SLOTS].start()


def grad_context_of(own, rest, wo, after):
    length = own.shape[0] + rest.shape[0]
    dma = pltpu.SemaphoreType.DMA
    slots = bf16(SLOTS, COLS, own.shape[1])
    scratch = [bf16(length, own.shape[1]), slots, dma((wo.shape[0] // COLS,)), dma((2,))]
    flops = 2 * length * wo.size
    outputs = [(length, wo.shape[0])]
    return call(context_gradient, (own, rest, far(wo)), outputs, scratch, flops, after, [ANY] * 3)[0]


def token_numbers(first, length, dim):
    place = lax.broadcasted_iota(jnp.int32, (length, length), dim) + first
    return jnp.where(place >= length, place - length, place)


def causal_bias(first, length):
    allowed = token_numbers(first, length, 1) >= token_numbers(first, length, 0)
    return jnp.where(allowed, 0.0, NEG_LARGE)


def stacked(ref, g):
    return jnp.concatenate([ref[:, part(h, HEAD_DIM)] for h in range(g * GROUP, (g + 1) * GROUP)], axis=0)


def causal_probs(keys, queries, bias):
    scores = nt(keys, queries) * SCALE + jnp.concatenate([bias[...]] * GROUP, axis=1)
    raised = jnp.exp(scores - jnp.max(scores, axis=0, keepdims=True))
    return raised * (1.0 / jnp.sum(raised, axis=0, keepdims=True))


def forward_layer(
    own, rest, gain, query_own, keyval_own, wo_far, *refs
):
    own_out, rest_out, wo, normed, query, keyval, context, bias, sems, out_sems = refs[-10:]
    weights = refs[:-10]
    row_count, width = own.shape
    length = row_count + rest.shape[0]
    groups = keyval.shape[1] // KEYVAL
    step_width = 1024
    rows = copy_rows([(query_own, query.at[:row_count, :]), (keyval_own, keyval.at[:row_count, :])], sems)
    parts = [part(step, step_width) for step in range(width // step_width)]
    out_copies = streamed([(wo_far.at[:, at], wo.at[i % SLOTS]) for i, at in enumerate(parts)], out_sems)
    norm_rows(rest, normed, gain[...])
    bias[...] = causal_bias(lax.axis_index("tensor") * row_count, length)
    project(normed, weights, query, keyval, row_count)
    for copy in rows:
        copy.wait()
    for g in range(groups):
        keys, values = keyval[:, part(g, HEAD_DIM)], keyval[:, part(groups + g, HEAD_DIM)]
        weights = causal_probs(keys, stacked(query, g), bias).astype(jnp.bfloat16)
        found = tn(weights, values).astype(jnp.bfloat16)
        for h in range(GROUP):
            context[:, part(g * GROUP + h, HEAD_DIM)] = found[part(h, length), :]
    for i, at in enumerate(parts):
        out_copies[i].wait()
        term = nn(context[...], wo[i % SLOTS])
        own_out[:, at] = (own[:, at].astype(jnp.float32) + term[:row_count]).astype(jnp.bfloat16)
        rest_out[:, at] = term[row_count:].astype(jnp.bfloat16)
        if i + SLOTS < len(parts):
            out_copies[i + SLOTS].start()


def backward_layer(
    own, rest, up_own, gain, query_own, keyval_own, grad_context, *refs
):
    own_out, rest_out, normed, query, keyval, grad_query, grad_keyval = refs[-12:-5]
    total, squares, products, bias, sems = refs[-5:]
    *wq, wkv = weights = refs[:-12]
    row_count, width = own.shape
    length = row_count + rest.shape[0]
    groups = keyval.shape[1] // KEYVAL
    rows = copy_rows([(query_own, query.at[:row_count, :]), (keyval_own, keyval.at[:row_count, :])], sems)
    norm_rows(rest, normed, gain[...])
    bias[...] = causal_bias(lax.axis_index("tensor") * row_count, length)
    project(normed, weights, query, keyval, row_count)
    for copy in rows:
        copy.wait()
    for g in range(groups):
        keys, values = keyval[:, part(g, HEAD_DIM)], keyval[:, part(groups + g, HEAD_DIM)]
        queries, above = stacked(query, g), stacked(grad_context, g)
        probs = causal_probs(keys, queries, bias)
        grad_value = nn(probs.astype(jnp.bfloat16), above)
        grad_prob = nt(values, above)
        mean_grad = jnp.sum(probs * grad_prob, axis=0, keepdims=True)
        grad_score = (probs * (grad_prob - mean_grad) * SCALE).astype(jnp.bfloat16)
        found = tn(grad_score, keys).astype(jnp.bfloat16)
        for h in range(GROUP):
            grad_query[:, part(g * GROUP + h, HEAD_DIM)] = found[part(h, length), :]
        grad_keyval[:, part(g, HEAD_DIM)] = nn(grad_score, queries).astype(jnp.bfloat16)
        grad_keyval[:, part(groups + g, HEAD_DIM)] = grad_value.astype(jnp.bfloat16)

    step_width = 512
    squares[...] = jnp.zeros_like(squares)
    products[...] = jnp.zeros_like(products)
    halves = ((own, 0, row_count), (rest, row_count, length))
    for step in range(width // step_width):
        at = part(step, step_width)
        term = nt(grad_keyval[...], wkv[at, :])
        for i, weight in enumerate(wq):
            term += nt(grad_query[:, part(i, weight.shape[1])], weight[at, :])
        term *= gain[:, at]
        total[:, at] = term
        for rows, start, stop in halves:
            values = rows[:, at].astype(jnp.float32)
            square, product = values * values, values * term[start:stop]
            lanes = [part(i, HEAD_DIM) for i in range(step_width // HEAD_DIM)]
            squares[start:stop, :] += sum(square[:, i] for i in lanes)
            products[start:stop, :] += sum(product[:, i] for i in lanes)

    def norm_grad(rows, at, among):
        factor = lax.rsqrt(jnp.sum(squares[among, :], axis=-1, keepdims=True) / width + EPSILON)
        mean = jnp.sum(products[among, :], axis=-1, keepdims=True) / width
        values = rows[at, :].astype(jnp.float32)
        return total[among, :] * factor - values * (factor * factor * factor * mean)

    @pl.loop(0, rest.shape[0] // ROW_STEP, unroll=2)
    def _(step):
        at = pl.ds(pl.multiple_of(step * ROW_STEP, ROW_STEP), ROW_STEP)
        among = pl.ds(pl.multiple_of(row_count + step * ROW_STEP, ROW_STEP), ROW_STEP)
        rest_out[at, :] = norm_grad(rest, at, among).astype(jnp.bfloat16)

    @pl.loop(0, row_count // ROW_STEP, unroll=2)
    def _(step):
        at = pl.ds(pl.multiple_of(step * ROW_STEP, ROW_STEP), ROW_STEP)
        own_out[at, :] = (up_own[at, :].astype(jnp.float32) + norm_grad(own, at, at)).astype(jnp.bfloat16)


def bf16(*shape):
    return pltpu.VMEM(shape, jnp.bfloat16)


def f32(*shape):
    return pltpu.VMEM(shape, jnp.float32)


def forward(own, rest, gain, projected, wo, weights, after):
    length, width = own.shape[0] + rest.shape[0], own.shape[1]
    queries, keyvals = (bf16(length, x.shape[1]) for x in projected)
    scratch = [
        bf16(SLOTS, wo.shape[0], 1024), bf16(*rest.shape), queries, keyvals, queries,
        f32(length, length), pltpu.SemaphoreType.DMA((2,)), pltpu.SemaphoreType.DMA((width // 1024,)),
    ]
    near = pl.BlockSpec(memory_space=pltpu.VMEM)
    specs = [near, near, near, ANY, ANY, ANY, *([near] * len(weights))]
    flops = 2 * rest.size * columns(weights) + 2 * length * wo.size
    inputs = (own, rest, gain, *projected, far(wo), *(held(x) for x in weights))
    return call(forward_layer, inputs, (own.shape, rest.shape), scratch, flops, after, specs)


def backward(own, rest, up_own, gain, projected, grad_context, weights, after):
    length, width = own.shape[0] + rest.shape[0], own.shape[1]
    queries, keyvals = (bf16(length, x.shape[1]) for x in projected)
    scratch = [
        bf16(*rest.shape), queries, keyvals, queries, keyvals,
        f32(length, width), f32(length, HEAD_DIM), f32(length, HEAD_DIM), f32(length, length),
        pltpu.SemaphoreType.DMA((2,)),
    ]
    near = pl.BlockSpec(memory_space=pltpu.VMEM)
    specs = [*([near] * 4), ANY, ANY, near, *([near] * len(weights))]
    flops = 2 * (rest.shape[0] + length) * width * columns(weights)
    inputs = (own, rest, up_own, gain, *projected, grad_context, *(held(x) for x in weights))
    return call(backward_layer, inputs, (own.shape, rest.shape), scratch, flops, after, specs)


def packing(marks, row_count):
    block_rows = row_count // marks.shape[0]
    rank = jnp.cumsum(marks) - 1
    place = jnp.repeat(rank, block_rows) * block_rows + jnp.arange(row_count) % block_rows
    chosen = jnp.repeat(marks, block_rows) == 1
    place = jnp.where(chosen, place, -1)
    slots = jnp.arange(MOST_EVICT * block_rows)
    return (place[None, :] == slots[:, None]).astype(jnp.bfloat16), chosen[:, None]


def others_rows(x):
    if lax.axis_size("tensor") == 2:
        return swapped(x)
    row_count = x.shape[0]
    rows = lax.all_gather(x, "tensor", axis=0, tiled=True)
    return jnp.roll(rows, -row_count * lax.axis_index("tensor"), axis=0)[row_count:]


def summed_and_moved(own, rest, by, term_first):
    if lax.axis_size("tensor") == 2:
        base, term = shifted(own, "section", by), crossed(rest, by)
        pair = (term, base) if term_first else (base, term)
        return (pair[0].astype(jnp.float32) + pair[1].astype(jnp.float32)).astype(jnp.bfloat16)
    rows = jnp.concatenate([own, rest], axis=0).astype(jnp.float32)
    rows = jnp.roll(rows, own.shape[0] * lax.axis_index("tensor"), axis=0)
    rows = lax.psum_scatter(rows, "tensor", scatter_dimension=0, tiled=True)
    return shifted(rows.astype(jnp.bfloat16), "section", by)


def local(
    activations,
    upstream_grad,
    stash_blocks,
    guest_blocks,
    norm_gain,
    query_weight,
    keyval_weight,
    output_weight,
    evict_marks,
):
    sections = lax.axis_size("section")
    section_index = lax.axis_index("section")
    current = activations[0]
    upstream = upstream_grad[0]
    stash_rows = stash_blocks[0]
    guest_rows = guest_blocks[0]
    row_count, model_width = current.shape
    upstream_rest = others_rows(upstream)

    own_marks = lax.dynamic_index_in_dim(evict_marks, section_index, 0, keepdims=False)
    mirror_marks = lax.dynamic_index_in_dim(
        evict_marks, sections - 1 - section_index, 0, keepdims=False
    )
    pack_own, own_mask = packing(own_marks, row_count)
    pack_mirror, _ = packing(mirror_marks, row_count)
    packed_shape = (pack_own.shape[0], model_width)
    pack_flops = 2 * pack_own.size * model_width
    guests = call(pack_rows, (pack_mirror, guest_rows), [packed_shape], [], pack_flops)[0]
    guests_back = mirrored(guests)
    chosen = own_mask.astype(jnp.int32)
    shapes = [current.shape, current.shape, packed_shape]
    current_copy, kept_rows, leaving = call(
        pack_and_copy, (pack_own, chosen, current), shapes, [], pack_flops, (guests,)
    )
    current_rest = others_rows(current_copy)
    arrived = mirrored(leaving)

    keyval_cols = keyval_weight.shape[3]
    keyval_flat = keyval_weight[0].reshape(model_width, 2 * keyval_cols)
    *weights, done = loaded(query_weight[0], keyval_flat, (current_copy,))
    wo = output_weight[0]

    grad_context = grad_context_of(upstream, upstream_rest, wo, (done,))
    unpack_inputs = (pack_own, chosen, guests_back, stash_rows)
    back_rows = call(
        unpack_rows, unpack_inputs, [current.shape], [], pack_flops, (grad_context,)
    )[0]
    back_rest = others_rows(back_rows)
    held_rows = tn(pack_mirror, arrived).astype(jnp.bfloat16)
    ahead = project_own(current, norm_gain, weights, (back_rows,))
    behind = project_own(back_rows, norm_gain, weights, ahead)

    ahead_own, ahead_rest = forward(current, current_rest, norm_gain, ahead, wo, weights, (*behind, arrived))
    next_input = summed_and_moved(ahead_own, ahead_rest, 1, True)
    grad_own, grad_rest = backward(
        back_rows, back_rest, upstream, norm_gain, behind, grad_context, weights, (ahead_rest,)
    )
    prev_grad = summed_and_moved(grad_own, grad_rest, -1, True)
    return (next_input[None], prev_grad[None], kept_rows[None], held_rows[None])


def solution(mesh):
    rows = P("section", "tensor", None)
    placed = (
        rows,
        rows,
        rows,
        rows,
        P("section", None),
        P("section", None, "tensor"),
        P("section", None, None, "tensor"),
        P("section", "tensor", None),
        P(),
    )
    return jax.shard_map(
        local, mesh=mesh, in_specs=placed, out_specs=(rows, rows, rows, rows), check_vma=False
    )
```

```python
import jax
import jax.numpy as jnp
from jax import lax
from jax.experimental import pallas as pl
from jax.experimental.pallas import tpu as pltpu
from jax.sharding import PartitionSpec as P

HEADS = 32
KV_HEADS = 8
HEAD_DIM = 128
GROUP = HEADS // KV_HEADS
MOST_EVICT = 8

EPSILON = 1e-05
NEG_LARGE = -1e30
SCALE = HEAD_DIM ** (-0.5)
ROW_STEP = 16
VMEM_BYTES = 16 * 1024 * 1024
SLOTS = 2


def shifted(x, axis, by):
    peers = lax.axis_size(axis)
    pairs = [(i, i + by) for i in range(peers) if 0 <= i + by < peers]
    return lax.ppermute(x, axis, pairs)


def crossed(x, by):
    peers = lax.axis_size("section")
    pairs = [
        (i * 2 + j, (i + by) * 2 + 1 - j) for i in range(peers) if 0 <= i + by < peers for j in (0, 1)
    ]
    return lax.ppermute(x, ("section", "tensor"), pairs)


def mirrored(x):
    peers = lax.axis_size("section")
    return lax.ppermute(x, "section", [(i, peers - 1 - i) for i in range(peers)])


def swapped(x):
    return lax.ppermute(x, "tensor", [(0, 1), (1, 0)])


def nn(a, b):
    return lax.dot_general(a, b, (((1,), (0,)), ((), ())), preferred_element_type=jnp.float32)


def nt(a, b):
    return lax.dot_general(a, b, (((1,), (1,)), ((), ())), preferred_element_type=jnp.float32)


def tn(a, b):
    return lax.dot_general(a, b, (((0,), (0,)), ((), ())), preferred_element_type=jnp.float32)


ANY = pl.BlockSpec(memory_space=pl.ANY)
KEYVAL = 2 * HEAD_DIM
COLS = GROUP * HEAD_DIM


def part(g, width):
    return slice(g * width, (g + 1) * width)


def call(kernel, inputs, outputs, scratch, flops, after=(), specs=None):
    near = pl.BlockSpec(memory_space=pltpu.VMEM)
    read = sum(x.size * x.dtype.itemsize for x in inputs)

    def body(*refs):
        kernel(*refs[: len(inputs)], *refs[len(inputs) + len(after) :])

    return pl.pallas_call(
        body,
        in_specs=[*(specs or [near] * len(inputs)), *([ANY] * len(after))],
        out_specs=[near] * len(outputs),
        out_shape=[
            jax.ShapeDtypeStruct(x, jnp.bfloat16) if isinstance(x, tuple) else x for x in outputs
        ],
        scratch_shapes=scratch,
        compiler_params=pltpu.CompilerParams(vmem_limit_bytes=VMEM_BYTES),
        cost_estimate=pl.CostEstimate(flops=flops, bytes_accessed=read, transcendentals=0),
        name=kernel.__name__,
    )(*inputs, *after)


def row_loop(row_count):
    steps = row_count // ROW_STEP
    return pl.loop(0, steps, unroll=4 if steps % 4 == 0 else 2)


def norm_rows(source, target, gain):
    @row_loop(source.shape[0])
    def _(step):
        at = pl.ds(pl.multiple_of(step * ROW_STEP, ROW_STEP), ROW_STEP)
        rows = source[at, :].astype(jnp.float32)
        factor = lax.rsqrt(jnp.mean(rows * rows, axis=-1, keepdims=True) + EPSILON)
        target[at, :] = (rows * factor * gain).astype(jnp.bfloat16)


def pack_and_copy(pack, chosen, rows, copied, kept, packed):
    copied[...] = rows[...]
    kept[...] = jnp.where(chosen[...] == 1, jnp.zeros_like(rows), rows[...])
    packed[...] = nn(pack[...], rows[...]).astype(jnp.bfloat16)


def pack_rows(pack, rows, out):
    out[...] = nn(pack[...], rows[...]).astype(jnp.bfloat16)


def unpack_rows(pack, chosen, rows, other, out):
    placed = tn(pack[...], rows[...]).astype(jnp.bfloat16)
    out[...] = jnp.where(chosen[...] == 1, placed, other[...])


def copy_rows(pairs, sems):
    copies = [pltpu.make_async_copy(far, near, sems.at[i]) for i, (far, near) in enumerate(pairs)]
    for copy in copies:
        copy.start()
    return copies


def streamed(pairs, sems):
    copies = [pltpu.make_async_copy(far, near, sems.at[i]) for i, (far, near) in enumerate(pairs)]
    for copy in copies[:SLOTS]:
        copy.start()
    return copies


def held(x):
    return pltpu.with_memory_space_constraint(x, pltpu.VMEM)


def far(x):
    return pltpu.with_memory_space_constraint(x, pltpu.HBM)


HELD_WIDTH = 1024


def load_weights(wq_far, wkv_far, *refs):
    *wq, wkv, done, sems = refs
    width = wq[0].shape[1]
    pairs = [(wq_far.at[:, part(i, width)], near) for i, near in enumerate(wq)]
    for copy in copy_rows([(wkv_far, wkv), *pairs], sems):
        copy.wait()
    done[...] = jnp.zeros_like(done)


def loaded(wq, wkv, after):
    count = max(1, wq.shape[1] // HELD_WIDTH)
    wq_part = pltpu.VMEM((wq.shape[0], wq.shape[1] // count), wq.dtype)
    outputs = [wq_part] * count + [pltpu.VMEM(wkv.shape, wkv.dtype), (16, HEAD_DIM)]
    scratch = [pltpu.SemaphoreType.DMA((count + 1,))]
    return call(load_weights, (far(wq), far(wkv)), outputs, scratch, 0, after, [ANY] * 2)


def project(normed, weights, query, keyval, start):
    *wq, wkv = weights
    keyval[start:, :] = nn(normed[...], wkv[...]).astype(jnp.bfloat16)
    for i, weight in enumerate(wq):
        query[start:, part(i, weight.shape[1])] = nn(normed[...], weight[...]).astype(jnp.bfloat16)


def own_projection(rows, gain, *refs):
    *weights, query, keyval, normed = refs
    norm_rows(rows, normed, gain[...])
    project(normed, weights, query, keyval, 0)


def columns(weights):
    return sum(x.shape[1] for x in weights)


def project_own(rows, gain, weights, after):
    outputs = [(rows.shape[0], columns(weights[:-1])), (rows.shape[0], columns(weights[-1:]))]
    flops = 2 * rows.size * columns(weights)
    inputs = (rows, gain, *(held(x) for x in weights))
    return call(own_projection, inputs, outputs, [bf16(*rows.shape)], flops, after)


def context_gradient(own, rest, wo_far, out, upstream, wo, sems, row_sems):
    row_count, groups = own.shape[0], out.shape[1] // COLS
    pairs = [(own, upstream.at[:row_count, :]), (rest, upstream.at[row_count:, :])]
    rows = copy_rows(pairs, row_sems)
    copies = streamed([(wo_far.at[part(g, COLS), :], wo.at[g % SLOTS]) for g in range(groups)], sems)
    for copy in rows:
        copy.wait()
    for g in range(groups):
        copies[g].wait()
        out[:, part(g, COLS)] = nt(upstream[...], wo[g % SLOTS]).astype(jnp.bfloat16)
        if g + SLOTS < groups:
            copies[g + SLOTS].start()


def grad_context_of(own, rest, wo, after):
    length = own.shape[0] + rest.shape[0]
    dma = pltpu.SemaphoreType.DMA
    slots = bf16(SLOTS, COLS, own.shape[1])
    scratch = [bf16(length, own.shape[1]), slots, dma((wo.shape[0] // COLS,)), dma((2,))]
    flops = 2 * length * wo.size
    outputs = [(length, wo.shape[0])]
    return call(context_gradient, (own, rest, far(wo)), outputs, scratch, flops, after, [ANY] * 3)[0]


def token_numbers(first, length, dim):
    place = lax.broadcasted_iota(jnp.int32, (length, length), dim) + first
    return jnp.where(place >= length, place - length, place)


def causal_bias(first, length):
    allowed = token_numbers(first, length, 1) >= token_numbers(first, length, 0)
    return jnp.where(allowed, 0.0, NEG_LARGE)


def stacked(ref, g):
    return jnp.concatenate([ref[:, part(h, HEAD_DIM)] for h in range(g * GROUP, (g + 1) * GROUP)], axis=0)


def causal_probs(keys, queries, bias):
    scores = nt(keys, queries) * SCALE + jnp.concatenate([bias[...]] * GROUP, axis=1)
    raised = jnp.exp(scores - jnp.max(scores, axis=0, keepdims=True))
    return raised * (1.0 / jnp.sum(raised, axis=0, keepdims=True))


def forward_layer(
    own, rest, gain, query_own, keyval_own, wo_far, *refs
):
    own_out, rest_out, wo, normed, query, keyval, context, bias, sems, out_sems = refs[-10:]
    weights = refs[:-10]
    row_count, width = own.shape
    length = row_count + rest.shape[0]
    groups = keyval.shape[1] // KEYVAL
    step_width = 1024
    rows = copy_rows([(query_own, query.at[:row_count, :]), (keyval_own, keyval.at[:row_count, :])], sems)
    parts = [part(step, step_width) for step in range(width // step_width)]
    out_copies = streamed([(wo_far.at[:, at], wo.at[i % SLOTS]) for i, at in enumerate(parts)], out_sems)
    norm_rows(rest, normed, gain[...])
    bias[...] = causal_bias(lax.axis_index("tensor") * row_count, length)
    project(normed, weights, query, keyval, row_count)
    for copy in rows:
        copy.wait()
    for g in range(groups):
        keys, values = keyval[:, part(g, HEAD_DIM)], keyval[:, part(groups + g, HEAD_DIM)]
        weights = causal_probs(keys, stacked(query, g), bias).astype(jnp.bfloat16)
        found = tn(weights, values).astype(jnp.bfloat16)
        for h in range(GROUP):
            context[:, part(g * GROUP + h, HEAD_DIM)] = found[part(h, length), :]
    for i, at in enumerate(parts):
        out_copies[i].wait()
        term = nn(context[...], wo[i % SLOTS])
        own_out[:, at] = (own[:, at].astype(jnp.float32) + term[:row_count]).astype(jnp.bfloat16)
        rest_out[:, at] = term[row_count:].astype(jnp.bfloat16)
        if i + SLOTS < len(parts):
            out_copies[i + SLOTS].start()


def backward_layer(
    own, rest, up_own, gain, query_own, keyval_own, grad_context, *refs
):
    own_out, rest_out, normed, query, keyval, grad_query, grad_keyval = refs[-12:-5]
    total, squares, products, bias, sems = refs[-5:]
    *wq, wkv = weights = refs[:-12]
    row_count, width = own.shape
    length = row_count + rest.shape[0]
    groups = keyval.shape[1] // KEYVAL
    rows = copy_rows([(query_own, query.at[:row_count, :]), (keyval_own, keyval.at[:row_count, :])], sems)
    norm_rows(rest, normed, gain[...])
    bias[...] = causal_bias(lax.axis_index("tensor") * row_count, length)
    project(normed, weights, query, keyval, row_count)
    for copy in rows:
        copy.wait()
    for g in range(groups):
        keys, values = keyval[:, part(g, HEAD_DIM)], keyval[:, part(groups + g, HEAD_DIM)]
        queries, above = stacked(query, g), stacked(grad_context, g)
        probs = causal_probs(keys, queries, bias)
        grad_value = nn(probs.astype(jnp.bfloat16), above)
        grad_prob = nt(values, above)
        mean_grad = jnp.sum(probs * grad_prob, axis=0, keepdims=True)
        grad_score = (probs * (grad_prob - mean_grad) * SCALE).astype(jnp.bfloat16)
        found = tn(grad_score, keys).astype(jnp.bfloat16)
        for h in range(GROUP):
            grad_query[:, part(g * GROUP + h, HEAD_DIM)] = found[part(h, length), :]
        grad_keyval[:, part(g, HEAD_DIM)] = nn(grad_score, queries).astype(jnp.bfloat16)
        grad_keyval[:, part(groups + g, HEAD_DIM)] = grad_value.astype(jnp.bfloat16)

    step_width = 512
    squares[...] = jnp.zeros_like(squares)
    products[...] = jnp.zeros_like(products)
    halves = ((own, 0, row_count), (rest, row_count, length))
    for step in range(width // step_width):
        at = part(step, step_width)
        term = nt(grad_keyval[...], wkv[at, :])
        for i, weight in enumerate(wq):
            term += nt(grad_query[:, part(i, weight.shape[1])], weight[at, :])
        term *= gain[:, at]
        total[:, at] = term
        for rows, start, stop in halves:
            values = rows[:, at].astype(jnp.float32)
            square, product = values * values, values * term[start:stop]
            lanes = [part(i, HEAD_DIM) for i in range(step_width // HEAD_DIM)]
            squares[start:stop, :] += sum(square[:, i] for i in lanes)
            products[start:stop, :] += sum(product[:, i] for i in lanes)

    def norm_grad(rows, at, among):
        factor = lax.rsqrt(jnp.sum(squares[among, :], axis=-1, keepdims=True) / width + EPSILON)
        mean = jnp.sum(products[among, :], axis=-1, keepdims=True) / width
        values = rows[at, :].astype(jnp.float32)
        return total[among, :] * factor - values * (factor * factor * factor * mean)

    @row_loop(rest.shape[0])
    def _(step):
        at = pl.ds(pl.multiple_of(step * ROW_STEP, ROW_STEP), ROW_STEP)
        among = pl.ds(pl.multiple_of(row_count + step * ROW_STEP, ROW_STEP), ROW_STEP)
        rest_out[at, :] = norm_grad(rest, at, among).astype(jnp.bfloat16)

    @row_loop(row_count)
    def _(step):
        at = pl.ds(pl.multiple_of(step * ROW_STEP, ROW_STEP), ROW_STEP)
        own_out[at, :] = (up_own[at, :].astype(jnp.float32) + norm_grad(own, at, at)).astype(jnp.bfloat16)


def bf16(*shape):
    return pltpu.VMEM(shape, jnp.bfloat16)


def f32(*shape):
    return pltpu.VMEM(shape, jnp.float32)


def forward(own, rest, gain, projected, wo, weights, after):
    length, width = own.shape[0] + rest.shape[0], own.shape[1]
    queries, keyvals = (bf16(length, x.shape[1]) for x in projected)
    scratch = [
        bf16(SLOTS, wo.shape[0], 1024), bf16(*rest.shape), queries, keyvals, queries,
        f32(length, length), pltpu.SemaphoreType.DMA((2,)), pltpu.SemaphoreType.DMA((width // 1024,)),
    ]
    near = pl.BlockSpec(memory_space=pltpu.VMEM)
    specs = [near, near, near, ANY, ANY, ANY, *([near] * len(weights))]
    flops = 2 * rest.size * columns(weights) + 2 * length * wo.size
    inputs = (own, rest, gain, *projected, far(wo), *(held(x) for x in weights))
    return call(forward_layer, inputs, (own.shape, rest.shape), scratch, flops, after, specs)


def backward(own, rest, up_own, gain, projected, grad_context, weights, after):
    length, width = own.shape[0] + rest.shape[0], own.shape[1]
    queries, keyvals = (bf16(length, x.shape[1]) for x in projected)
    scratch = [
        bf16(*rest.shape), queries, keyvals, queries, keyvals,
        f32(length, width), f32(length, HEAD_DIM), f32(length, HEAD_DIM), f32(length, length),
        pltpu.SemaphoreType.DMA((2,)),
    ]
    near = pl.BlockSpec(memory_space=pltpu.VMEM)
    specs = [*([near] * 4), ANY, ANY, near, *([near] * len(weights))]
    flops = 2 * (rest.shape[0] + length) * width * columns(weights)
    inputs = (own, rest, up_own, gain, *projected, grad_context, *(held(x) for x in weights))
    return call(backward_layer, inputs, (own.shape, rest.shape), scratch, flops, after, specs)


def packing(marks, row_count):
    block_rows = row_count // marks.shape[0]
    rank = jnp.cumsum(marks) - 1
    place = jnp.repeat(rank, block_rows) * block_rows + jnp.arange(row_count) % block_rows
    chosen = jnp.repeat(marks, block_rows) == 1
    place = jnp.where(chosen, place, -1)
    slots = jnp.arange(MOST_EVICT * block_rows)
    return (place[None, :] == slots[:, None]).astype(jnp.bfloat16), chosen[:, None]


def others_rows(x):
    if lax.axis_size("tensor") == 2:
        return swapped(x)
    row_count = x.shape[0]
    rows = lax.all_gather(x, "tensor", axis=0, tiled=True)
    return jnp.roll(rows, -row_count * lax.axis_index("tensor"), axis=0)[row_count:]


def summed_and_moved(own, rest, by, term_first):
    if lax.axis_size("tensor") == 2:
        base, term = shifted(own, "section", by), crossed(rest, by)
        pair = (term, base) if term_first else (base, term)
        return (pair[0].astype(jnp.float32) + pair[1].astype(jnp.float32)).astype(jnp.bfloat16)
    rows = jnp.concatenate([own, rest], axis=0).astype(jnp.float32)
    rows = jnp.roll(rows, own.shape[0] * lax.axis_index("tensor"), axis=0)
    rows = lax.psum_scatter(rows, "tensor", scatter_dimension=0, tiled=True)
    return shifted(rows.astype(jnp.bfloat16), "section", by)


def local(
    activations,
    upstream_grad,
    stash_blocks,
    guest_blocks,
    norm_gain,
    query_weight,
    keyval_weight,
    output_weight,
    evict_marks,
):
    sections = lax.axis_size("section")
    section_index = lax.axis_index("section")
    current = activations[0]
    upstream = upstream_grad[0]
    stash_rows = stash_blocks[0]
    guest_rows = guest_blocks[0]
    row_count, model_width = current.shape
    upstream_rest = others_rows(upstream)

    own_marks = lax.dynamic_index_in_dim(evict_marks, section_index, 0, keepdims=False)
    mirror_marks = lax.dynamic_index_in_dim(
        evict_marks, sections - 1 - section_index, 0, keepdims=False
    )
    pack_own, own_mask = packing(own_marks, row_count)
    pack_mirror, _ = packing(mirror_marks, row_count)
    packed_shape = (pack_own.shape[0], model_width)
    pack_flops = 2 * pack_own.size * model_width
    guests = call(pack_rows, (pack_mirror, guest_rows), [packed_shape], [], pack_flops)[0]
    guests_back = mirrored(guests)
    chosen = own_mask.astype(jnp.int32)
    shapes = [current.shape, current.shape, packed_shape]
    current_copy, kept_rows, leaving = call(
        pack_and_copy, (pack_own, chosen, current), shapes, [], pack_flops, (guests,)
    )
    current_rest = others_rows(current_copy)
    arrived = mirrored(leaving)

    keyval_cols = keyval_weight.shape[3]
    keyval_flat = keyval_weight[0].reshape(model_width, 2 * keyval_cols)
    *weights, done = loaded(query_weight[0], keyval_flat, (current_copy,))
    wo = output_weight[0]

    grad_context = grad_context_of(upstream, upstream_rest, wo, (done,))
    unpack_inputs = (pack_own, chosen, guests_back, stash_rows)
    back_rows = call(
        unpack_rows, unpack_inputs, [current.shape], [], pack_flops, (grad_context,)
    )[0]
    back_rest = others_rows(back_rows)
    held_rows = tn(pack_mirror, arrived).astype(jnp.bfloat16)
    ahead = project_own(current, norm_gain, weights, (back_rows,))
    behind = project_own(back_rows, norm_gain, weights, ahead)

    ahead_own, ahead_rest = forward(current, current_rest, norm_gain, ahead, wo, weights, (*behind, arrived))
    next_input = summed_and_moved(ahead_own, ahead_rest, 1, True)
    grad_own, grad_rest = backward(
        back_rows, back_rest, upstream, norm_gain, behind, grad_context, weights, (ahead_rest,)
    )
    prev_grad = summed_and_moved(grad_own, grad_rest, -1, True)
    return (next_input[None], prev_grad[None], kept_rows[None], held_rows[None])


def solution(mesh):
    rows = P("section", "tensor", None)
    placed = (
        rows,
        rows,
        rows,
        rows,
        P("section", None),
        P("section", None, "tensor"),
        P("section", None, None, "tensor"),
        P("section", "tensor", None),
        P(),
    )
    return jax.shard_map(
        local, mesh=mesh, in_specs=placed, out_specs=(rows, rows, rows, rows), check_vma=False
    )
```
